32 devices in a mesh: group: 2 (over y), dp: 4 (over z), tensor: 4 (over x, core).
Axes of the slice: x: 2, y: 2, z: 4, core: 2. Of those that a mesh axis runs over, the one named last changes fastest.
Arguments:
- attended: bfloat16 [1024, 8192], P(('group', 'dp'), 'tensor'), parts along dimension 0, may hold values from -6 to 6
- hidden: bfloat16 [1024, 8192], P(('group', 'dp'), 'tensor'), parts along dimension 0, may hold values from -6 to 6
- output_weight: bfloat16 [8192, 8192], P('tensor'), may hold values from -0.09375 to 0.09375
- low_rank_shrink: bfloat16 [64, 64, 8192], P(('group', 'dp'), None, 'tensor'), parts along dimension 0, may hold values from -0.0625 to 0.0625
- low_rank_expand: bfloat16 [64, 64, 8192], P(('group', 'dp'), None, 'tensor'), parts along dimension 0, may hold values from -0.75 to 0.75
- row_adapter_index: int32 [1024, 1], P(('group', 'dp')), parts along dimension 0, may hold values from 0 to 31; in each aligned block of 128 rows (0 to 127, 128 to 255, ...) at most 8 rows name the same one
- adapter_store_slot: int32 [64], P('group'), parts along dimension 0, may hold values from 0 to 31, each once
Outputs:
- mixed: bfloat16 [1024, 8192], P(('group', 'dp'), 'tensor'), parts along dimension 0
The draws below stay inside these ranges and needn't reach their ends.
There are 2 independent parts, one for each index of `group`. The reference program is written for one: setup_inputs(seed, part) draws one part's arguments, and reference() takes and returns one part's arrays. A program takes and returns all parts, laid end to end along the dimension named above; an argument that names none is the same for every part. Nothing has to cross between parts.
Inputs may be any that keep to these rules, and one draw needn't show every extreme that they name: `row_adapter_index`: in the rows of one dp index (aligned blocks of 128 rows) each adapter is named at most 8 times, a bound that some block reaches. A permutation: adapter a lies in store slot adapter_store_slot[a], held by dp index adapter_store_slot[a] // 8.
All inputs are finite; a program needn't handle non-finite values.
Results may differ from the reference program's by a relative error of at most 0.0036.
Values may be sent and summed in bfloat16 or wider, within the bound.
A program may use at most 128 MiB of HBM per device.

```python
import math
import jax
import jax.numpy as jnp
import numpy as np

MODEL_WIDTH = 8192
ADAPTER_RANK = 64
ADAPTER_ROW_CAP = 8
ROWS_DP = 128
ROWS = 512
ADAPTER_TOTAL = 32
N_DP = 4


def spiked(entries, stream_key, source, target, blocks, factor):
    def block_of(dim):
        return (jnp.arange(entries.shape[dim]) // (entries.shape[dim] // blocks)).reshape((-1,) + (1,) * (entries.ndim - 1 - dim))

    first = jax.random.permutation(stream_key, blocks)[block_of(target)]
    far = (block_of(target) + blocks // 2) % blocks
    return jnp.where((block_of(source) == first) | (block_of(source) == far), factor * entries, entries)


def level_of(stream_key, shape, shards, least, largest):
    def one(dim, blocks):
        steps = jax.random.uniform(jax.random.fold_in(jax.random.fold_in(stream_key, 6), dim), (blocks,), jnp.float32, least / len(shards), largest / len(shards))
        return jnp.repeat(jnp.exp(steps), shape[dim] // blocks).reshape((-1,) + (1,) * (len(shape) - dim - 1))

    gain = one(*shards[0])
    for cut in shards[1:]:
        gain = gain * one(*cut)
    return gain


def shared_out(rng, own, number, rows, amount, top, bound, slope):
    order = jax.random.permutation(rng, amount)
    packed, common = load_shares(amount, rows * top, bound, slope, True), load_shares(amount, rows * top, bound, slope, False)
    places = jnp.arange(amount)

    def named(sizes, offset_by):
        used = int((sizes > 0).sum())
        fixed = max(1, used // 4)
        moved = fixed + (places - fixed + offset_by * (used - fixed)) % max(1, amount - fixed)
        return jnp.zeros((amount,), jnp.int32).at[order[jnp.where(places < fixed, places, moved)]].set(jnp.asarray(sizes, jnp.int32))

    sizes = jnp.where(number % 4 == 0, named(packed, number // 4), named(common, number - number // 4 - 1))
    mixed = jax.random.permutation(jax.random.fold_in(own, 3), amount)
    donor, taker = mixed[0:amount // 2 * 2:2], mixed[1:amount // 2 * 2:2]
    slack = jnp.minimum(sizes[donor] - 1, bound - sizes[taker]) // 2
    slack = jnp.where((donor == order[0]) | (taker == order[0]) | (sizes[taker] == 0), 0, jnp.maximum(slack, 0))
    moved = jax.random.randint(jax.random.fold_in(own, 4), (amount // 2,), 0, 1 << 20) % (slack + 1)
    sizes = sizes.at[donor].add(-moved).at[taker].add(moved)
    members = jnp.searchsorted(jnp.cumsum(sizes), jnp.arange(rows * top), side="right").astype(jnp.int32)
    table = members.reshape(top, rows).T
    table = table[jax.random.permutation(jax.random.fold_in(own, 1), rows)]
    offset_by = jax.random.randint(jax.random.fold_in(own, 2), (rows, 1), 0, top)
    return jnp.take_along_axis(table, (jnp.arange(top)[None, :] + offset_by) % top, axis=1)


def load_shares(amount, total, bound, skew, full):
    portions = [(1 << 20) // math.isqrt(standing ** skew) + 1 for standing in range(1, amount + 1)]
    largest = bound if full else min(bound, max(-(-total // amount), total * portions[0] // sum(portions)))
    least = 1 if total - largest >= amount - 1 else 0
    given, surplus = [largest] + [least] * (amount - 1), total - largest - least * (amount - 1)
    while surplus > 0:
        movable = [i for i in range(1, amount) if given[i] < largest] or [i for i in range(1, amount) if given[i] < bound]
        whole, remaining = sum([portions[i] for i in movable]), surplus
        for i in movable:
            more = min(bound - given[i], max(1, remaining * portions[i] // whole), surplus)
            given[i] = given[i] + more
            surplus = surplus - more
    return np.array(given)


def bell_draw(key, shape, deviation, bound, split=(), held_as=jnp.bfloat16):
    values = deviation * jax.random.normal(key, shape, jnp.float32)
    if split:
        values = values * level_of(key, shape, split, -0.22, 0.18)
    return jnp.clip(values, -bound, bound).astype(held_as)


def noise_with(key, shape, scale, bound, pieces, heavy, kind=jnp.bfloat16):
    array = scale * jax.random.normal(key, shape, jnp.float32)
    if pieces:
        array = array * level_of(key, shape, pieces, -0.22, 0.18)
    return jnp.clip(spiked(array, jax.random.fold_in(key, 3), *heavy), -bound, bound).astype(kind)


def setup_inputs(seed: int = 0, part: int = 0) -> dict:
    seeds = jax.random.split(jax.random.key(seed), 8)
    own_keys = jax.random.split(jax.random.fold_in(seeds[7], part), 8)
    attended = bell_draw(own_keys[0], (ROWS, MODEL_WIDTH), 1.0, 6.0, ((0, 4), (1, 4)))
    hidden = bell_draw(own_keys[1], (ROWS, MODEL_WIDTH), 1.0, 6.0, ((0, 4), (1, 4)))
    output_weight = noise_with(seeds[2], (MODEL_WIDTH, MODEL_WIDTH), MODEL_WIDTH ** -0.5, 0.09375, ((0, 4),), (0, 1, 4, 2.0))
    low_rank_shrink = bell_draw(own_keys[3], (ADAPTER_TOTAL, ADAPTER_RANK, MODEL_WIDTH), MODEL_WIDTH ** -0.5, 0.0625, ((0, 4), (2, 4)))
    low_rank_expand = bell_draw(own_keys[4], (ADAPTER_TOTAL, ADAPTER_RANK, MODEL_WIDTH), ADAPTER_RANK ** -0.5, 0.75, ((0, 4), (2, 4)))
    row_adapter_index_keys = jax.random.split(jax.random.fold_in(own_keys[5], 1), ROWS // ROWS_DP)
    row_adapter_index_turns = jax.random.permutation(jax.random.fold_in(own_keys[5], 3), ROWS // ROWS_DP)
    row_adapter_index = jax.vmap(lambda own, number: shared_out(jax.random.fold_in(own_keys[5], 2), own, number, ROWS_DP, ADAPTER_TOTAL, 1, ADAPTER_ROW_CAP, 2))(row_adapter_index_keys, row_adapter_index_turns).reshape((ROWS, 1))
    adapter_store_slot = jax.random.permutation(own_keys[6], ADAPTER_TOTAL).astype(jnp.int32)
    return dict(attended=attended, hidden=hidden, output_weight=output_weight, low_rank_shrink=low_rank_shrink, low_rank_expand=low_rank_expand, row_adapter_index=row_adapter_index, adapter_store_slot=adapter_store_slot)


def reference(attended, hidden, output_weight, low_rank_shrink, low_rank_expand, row_adapter_index, adapter_store_slot):
    base_projection_sum = jnp.dot(attended, output_weight, preferred_element_type=jnp.float32)
    row_adapter = row_adapter_index[:, 0].astype(jnp.int32)
    row_total = row_adapter.shape[0]
    per_block = row_total // N_DP
    blocks = row_adapter.reshape(N_DP, per_block)
    earlier = jnp.tri(per_block, k=-1, dtype=bool)
    same_adapter = blocks[:, :, None] == blocks[:, None, :]
    row_place = jnp.sum(same_adapter & earlier[None], axis=2).astype(jnp.int32).reshape(row_total)
    row_shard = (jnp.arange(row_total, dtype=jnp.int32) // per_block).astype(jnp.int32)
    row_slot = adapter_store_slot[row_adapter].astype(jnp.int32)
    target_rows = (row_slot * (N_DP * ADAPTER_ROW_CAP) + row_shard * ADAPTER_ROW_CAP + row_place).astype(jnp.int32)
    store_slot_count = ADAPTER_TOTAL * N_DP * ADAPTER_ROW_CAP
    holding_buffer = jnp.zeros((store_slot_count, MODEL_WIDTH), jnp.bfloat16).at[target_rows].set(attended)
    holding_buffer = holding_buffer.reshape(ADAPTER_TOTAL, N_DP * ADAPTER_ROW_CAP, MODEL_WIDTH)
    shrunk_rows = jnp.einsum("fex,fyx->fey", holding_buffer.astype(jnp.float32), low_rank_shrink.astype(jnp.float32)).astype(jnp.bfloat16)
    expanded_rows = jnp.einsum("zxb,zbl->zxl", shrunk_rows.astype(jnp.float32), low_rank_expand.astype(jnp.float32)).astype(jnp.bfloat16)
    low_rank_delta = expanded_rows.reshape(store_slot_count, MODEL_WIDTH)[target_rows]
    return (hidden.astype(jnp.float32) + base_projection_sum + low_rank_delta.astype(jnp.float32)).astype(jnp.bfloat16)
```

```python
import functools

import jax
import jax.numpy as jnp
from jax import lax
from jax.experimental import pallas as pl
from jax.experimental.pallas import tpu as pltpu
from jax.sharding import PartitionSpec as P

MESH = pl.DeviceIdType.MESH
ADAPTER_ROW_CAP = 8
CHUNKS = 2
RING = 4
F32 = jnp.float32
BF16 = jnp.bfloat16


def kernel(
    n_dp, n_t, cap,
    att, idx, slots, hid_hbm, w_hbm, shr_hbm, exp_hbm,
    out,
    sel, hold, recv, meta, metar, slc, zs, zr, dl, ret,
    wbuf, psend, precv, own, xsend, xrecv, hid, shr, exp,
    w_sem, in_sem, f_ss, f_rs, m_ss, m_rs, z_ss, z_rs, r_ss, r_rs, p_ss, p_rs, x_ss, x_rs,
):
    rows, width = att.shape
    store = shr.shape[0]
    n_x = n_t // 2
    n_j, tile = own.shape[1], own.shape[3]
    block = n_j * tile
    per_slot = store // (cap // ADAPTER_ROW_CAP)
    n_slots = store // per_slot
    ch = cap // CHUNKS
    wide = n_dp * ch
    d = lax.axis_index("dp")
    t = lax.axis_index("tensor")
    x, c = t // 2, lax.rem(t, 2)
    sibling = {"tensor": x * 2 + (1 - c)}

    def dp_at(off):
        return {"dp": lax.rem(d + off, n_dp)}

    def t_at(off):
        return {"tensor": lax.rem(t + off, n_t)}

    def w_copy(g, slot):
        i, h, j = g // (2 * n_j), lax.rem(g // n_j, 2), lax.rem(g, n_j)
        core = jnp.where(h == 0, 1 - c, c)
        dest = lax.rem(x + 1 + i, n_x) * 2 + core
        start = pl.multiple_of(dest * block + j * tile, tile)
        return pltpu.make_async_copy(w_hbm.at[:, pl.ds(start, tile)], wbuf.at[slot], w_sem.at[slot])

    barrier = pltpu.get_barrier_semaphore()
    for off in range(1, n_dp):
        pl.semaphore_signal(barrier, inc=1, device_id=dp_at(off), device_id_type=MESH)
    for off in range(1, n_t):
        pl.semaphore_signal(barrier, inc=1, device_id=t_at(off), device_id_type=MESH)

    for g in range(RING):
        w_copy(jnp.int32(g), g).start()
    loads = [
        pltpu.make_async_copy(shr_hbm, shr, in_sem.at[0]),
        pltpu.make_async_copy(exp_hbm, exp, in_sem.at[1]),
        pltpu.make_async_copy(hid_hbm, hid, in_sem.at[2]),
    ]
    for load in loads:
        load.start()

    n_ad = slots.shape[1]
    match = idx[...] == lax.broadcasted_iota(jnp.int32, (rows, n_ad), 1)
    slot = jnp.sum(jnp.where(match, slots[...].astype(F32), 0.0), axis=1, keepdims=True)
    owner = jnp.zeros((rows, 1), F32)
    for o in range(1, n_dp):
        owner = owner + jnp.where(slot >= float(o * n_slots), 1.0, 0.0)
    local = slot - owner * n_slots
    rel = owner - d.astype(F32)
    rel = jnp.where(rel < 0, rel + n_dp, rel)
    lane = lax.broadcasted_iota(jnp.int32, (rows, 128), 1).astype(F32)
    to_owner = lane == rel
    before = (
        lax.broadcasted_iota(jnp.int32, (rows, rows), 1)
        < lax.broadcasted_iota(jnp.int32, (rows, rows), 0)
    )
    earlier = jnp.dot(
        jnp.where(before, 1.0, 0.0).astype(BF16),
        jnp.where(to_owner, 1.0, 0.0).astype(BF16),
        preferred_element_type=F32,
    )
    place = jnp.sum(jnp.where(to_owner, earlier, 0.0), axis=1, keepdims=True)
    target = place + rel * ch
    for k in range(1, CHUNKS):
        target = target + jnp.where(place >= float(k * ch), float(wide - ch), 0.0)
    columns = lax.broadcasted_iota(jnp.int32, (rows, CHUNKS * wide), 1).astype(F32)
    sel[...] = jnp.where(columns == target, 1.0, 0.0).astype(BF16)
    for off in range(n_dp):
        here = jnp.where((lane == place) & (rel == float(off)), local, 0.0)
        row = jnp.broadcast_to(jnp.sum(here, axis=0, keepdims=True), (8, 128))
        if off == 0:
            metar[0] = row
        else:
            meta[off] = row

    fw = min(512, width)
    for k in range(CHUNKS):
        for f in range(width // fw):
            cols = pl.ds(f * fw, fw)
            part = lax.dot_general(
                sel[:, k * wide : (k + 1) * wide], att[:, cols], (((0,), (0,)), ((), ())),
                preferred_element_type=F32,
            ).astype(BF16)
            recv[k, pl.ds(0, ch), cols] = part[:ch]
            hold[k, pl.ds(ch, wide - ch), cols] = part[ch:]

    pl.semaphore_wait(barrier, n_dp + n_t - 2)

    order = sorted(range(1, n_dp), key=lambda off: -min(off, n_dp - off))

    def f_copy(k, off):
        return pltpu.make_async_remote_copy(
            src_ref=hold.at[k, pl.ds(off * ch, ch)], dst_ref=recv.at[k, pl.ds(off * ch, ch)],
            send_sem=f_ss.at[k, off], recv_sem=f_rs.at[k, off],
            device_id=dp_at(off), device_id_type=MESH,
        )

    def m_copy(off):
        return pltpu.make_async_remote_copy(
            src_ref=meta.at[off], dst_ref=metar.at[off],
            send_sem=m_ss.at[off], recv_sem=m_rs.at[off],
            device_id=dp_at(off), device_id_type=MESH,
        )

    def z_copy(k, off):
        return pltpu.make_async_remote_copy(
            src_ref=zs.at[k], dst_ref=zr.at[k, off],
            send_sem=z_ss.at[k, off], recv_sem=z_rs.at[k, off],
            device_id=t_at(off), device_id_type=MESH,
        )

    def r_copy(k, off):
        return pltpu.make_async_remote_copy(
            src_ref=dl.at[k, pl.ds(off * ch, ch)], dst_ref=ret.at[k, pl.ds(off * ch, ch)],
            send_sem=r_ss.at[k, off], recv_sem=r_rs.at[k, off],
            device_id=dp_at(n_dp - off), device_id_type=MESH,
        )

    def p_copy(i):
        return pltpu.make_async_remote_copy(
            src_ref=psend.at[i], dst_ref=precv.at[i],
            send_sem=p_ss.at[i], recv_sem=p_rs.at[i],
            device_id=sibling, device_id_type=MESH,
        )

    def x_copy(i):
        return pltpu.make_async_remote_copy(
            src_ref=xsend.at[i], dst_ref=xrecv.at[i],
            send_sem=x_ss.at[i], recv_sem=x_rs.at[i],
            device_id={"tensor": lax.rem(x + 1 + i, n_x) * 2 + c}, device_id_type=MESH,
        )

    for off in order:
        m_copy(off).start()
    for k in range(CHUNKS):
        for off in order:
            f_copy(k, off).start()

    tiles = n_t * n_j

    def product(g):
        at = lax.rem(g, RING)
        w_copy(g, at).wait()
        part = jnp.dot(att[...], wbuf[at], preferred_element_type=F32)

        return part, at

    def refill(g, at):
        @pl.when(g + RING < tiles)
        def _():
            w_copy(g + RING, at).start()

    def blocks(i):
        def first(j, carry):
            g = i * 2 * n_j + j
            part, at = product(g)
            psend[i, j] = part
            refill(g, at)
            return carry

        lax.fori_loop(0, n_j, first, 0)
        p_copy(i).start()

        def second(j, carry):
            g = i * 2 * n_j + n_j + j
            part, at = product(g)
            own[i, j] = part
            refill(g, at)
            return carry

        lax.fori_loop(0, n_j, second, 0)
        p_copy(i).wait_recv()

    def far(i, carry):
        blocks(i)

        def add(j, inner):
            xsend[i, j] = (own[i, j] + precv[i, j]).astype(BF16)
            return inner

        lax.fori_loop(0, n_j, add, 0)
        x_copy(i).start()
        return carry

    lax.fori_loop(0, n_x - 1, far, 0)
    blocks(jnp.int32(n_x - 1))

    for load in loads:
        load.wait()
    for off in order:
        m_copy(off).wait_recv()
    n_q = store // 128
    per = 128 // per_slot
    half = lax.broadcasted_iota(jnp.int32, (wide, 128), 1) // per_slot
    half = half.astype(F32)
    for k in range(CHUNKS):
        r_i = lax.broadcasted_iota(jnp.int32, (ch, 128), 0) + k * ch
        pick = lax.broadcasted_iota(jnp.int32, (ch, 128), 1) == r_i
        for off in range(n_dp):
            col = jnp.sum(jnp.where(pick, metar[off, 0:1, :], 0.0), axis=1, keepdims=True)
            slc[k, pl.ds(off * ch, ch)] = jnp.broadcast_to(col, (ch, 128))

    for k in range(CHUNKS):
        for off in order:
            f_copy(k, off).wait_recv()
        y = lax.dot_general(
            recv[k], shr[...], (((1,), (1,)), ((), ())), preferred_element_type=F32
        )
        z = jnp.zeros((wide, 128), F32)
        for q in range(n_q):
            z = z + jnp.where(slc[k] == half + float(q * per), y[:, q * 128 : (q + 1) * 128], 0.0)
        zs[k] = z
        for off in range(1, n_t):
            z_copy(k, off).start()
        for off in range(1, n_t):
            z_copy(k, off).wait_recv()
        total = zs[k]
        for off in range(1, n_t):
            total = total + zr[k, off]
        mixed = [
            jnp.where(slc[k] == half + float(q * per), total, 0.0).astype(BF16) for q in range(n_q)
        ]
        lhs = jnp.concatenate(mixed, axis=1)
        for f in range(width // fw):
            cols = pl.ds(f * fw, fw)
            part = jnp.dot(lhs, exp[:, cols], preferred_element_type=F32).astype(BF16)
            ret[k, pl.ds(0, ch), cols] = part[:ch]
            dl[k, pl.ds(ch, wide - ch), cols] = part[ch:]
        for off in order:
            r_copy(k, off).start()

    for i in range(n_x - 1):
        x_copy(i).wait_recv()
    for j in range(n_j):
        cols = pl.ds(j * tile, tile)
        total = own[n_x - 1, j] + precv[n_x - 1, j]
        for i in range(n_x - 1):
            total = total + xrecv[i, j].astype(F32)
        own[n_x - 1, j] = hid[:, cols].astype(F32) + total

    for k in range(CHUNKS):
        for off in order:
            r_copy(k, off).wait_recv()
    for j in range(n_j):
        cols = pl.ds(j * tile, tile)
        delta = own[n_x - 1, j]
        for k in range(CHUNKS):
            delta = delta + jnp.dot(
                sel[:, k * wide : (k + 1) * wide], ret[k, :, cols], preferred_element_type=F32
            )
        out[:, cols] = delta.astype(BF16)

    for off in order:
        m_copy(off).wait_send()
        for k in range(CHUNKS):
            f_copy(k, off).wait_send()
            r_copy(k, off).wait_send()
    for k in range(CHUNKS):
        for off in range(1, n_t):
            z_copy(k, off).wait_send()
    for i in range(n_x):
        p_copy(i).wait_send()
    for i in range(n_x - 1):
        x_copy(i).wait_send()


def solution(mesh):
    n_dp, n_t = mesh.shape["dp"], mesh.shape["tensor"]
    n_x = n_t // 2

    def per_device(attended, hidden, weight, shrink, expand, row_adapter, store_slot):
        rows, width = attended.shape
        n_slots, rank, _ = shrink.shape
        cap = n_slots * ADAPTER_ROW_CAP
        ch = cap // CHUNKS
        wide = n_dp * ch
        depth, total = weight.shape
        block = total // n_t
        tile = min(512, block)
        n_j = block // tile
        any_space = pl.BlockSpec(memory_space=pl.ANY)
        vmem = pl.BlockSpec(memory_space=pltpu.VMEM)
        dma = pltpu.SemaphoreType.DMA
        return pl.pallas_call(
            functools.partial(kernel, n_dp, n_t, cap),
            out_shape=jax.ShapeDtypeStruct((rows, width), BF16),
            in_specs=[vmem, vmem, vmem, any_space, any_space, any_space, any_space],
            out_specs=vmem,
            scratch_shapes=[
                pltpu.VMEM((rows, CHUNKS * wide), BF16),
                pltpu.VMEM((CHUNKS, wide, width), BF16),
                pltpu.VMEM((CHUNKS, wide, width), BF16),
                pltpu.VMEM((n_dp, 8, 128), F32),
                pltpu.VMEM((n_dp, 8, 128), F32),
                pltpu.VMEM((CHUNKS, wide, 128), F32),
                pltpu.VMEM((CHUNKS, wide, 128), F32),
                pltpu.VMEM((CHUNKS, n_t, wide, 128), F32),
                pltpu.VMEM((CHUNKS, wide, width), BF16),
                pltpu.VMEM((CHUNKS, wide, width), BF16),
                pltpu.VMEM((RING, depth, tile), BF16),
                pltpu.VMEM((n_x, n_j, rows, tile), F32),
                pltpu.VMEM((n_x, n_j, rows, tile), F32),
                pltpu.VMEM((n_x, n_j, rows, tile), F32),
                pltpu.VMEM((n_x - 1, n_j, rows, tile), BF16),
                pltpu.VMEM((n_x - 1, n_j, rows, tile), BF16),
                pltpu.VMEM((rows, width), BF16),
                pltpu.VMEM((n_slots * rank, width), BF16),
                pltpu.VMEM((n_slots * rank, width), BF16),
                dma((RING,)), dma((3,)),
                dma((CHUNKS, n_dp)), dma((CHUNKS, n_dp)), dma((n_dp,)), dma((n_dp,)),
                dma((CHUNKS, n_t)), dma((CHUNKS, n_t)), dma((CHUNKS, n_dp)), dma((CHUNKS, n_dp)),
                dma((n_x,)), dma((n_x,)), dma((n_x,)), dma((n_x,)),
            ],
            compiler_params=pltpu.CompilerParams(
                collective_id=0, has_side_effects=True, vmem_limit_bytes=48 * 1024 * 1024
            ),
        )(
            attended, row_adapter, store_slot.reshape(1, -1), hidden, weight,
            shrink.reshape(n_slots * rank, width), expand.reshape(n_slots * rank, width),
        )

    placed = (
        P(("group", "dp"), "tensor"),
        P(("group", "dp"), "tensor"),
        P("tensor", None),
        P(("group", "dp"), None, "tensor"),
        P(("group", "dp"), None, "tensor"),
        P(("group", "dp"), None),
        P("group"),
    )
    return jax.shard_map(
        per_device,
        mesh=mesh,
        in_specs=placed,
        out_specs=P(("group", "dp"), "tensor"),
        check_vma=False,
    )
```

```python
import functools

import jax
import jax.numpy as jnp
from jax import lax
from jax.experimental import pallas as pl
from jax.experimental.pallas import tpu as pltpu
from jax.sharding import PartitionSpec as P

MESH = pl.DeviceIdType.MESH
ADAPTER_ROW_CAP = 8
RING = 4
F32 = jnp.float32
BF16 = jnp.bfloat16


def kernel(
    n_group, n_dp, n_t, n_slots, sizes, flagged,
    idx, slots, att_hbm, hid_hbm, w_hbm, shr_hbm, exp_hbm,
    out, over,
    att, flags, sel, hold, recv, meta, metar, slc, zs, zr, dl, ret,
    wbuf, psend, precv, own, xsend, xrecv, hid, shr, exp,
    w_sem, in_sem, f_ss, f_rs, m_ss, m_rs, z_ss, z_rs, r_ss, r_rs, p_ss, p_rs, x_ss, x_rs, o_ss, o_rs,
):
    rows, width = att.shape
    store = shr.shape[0]
    n_x = n_t // 2
    n_j, tile = own.shape[1], own.shape[3]
    block = n_j * tile
    per_slot = store // n_slots
    cap = sum(sizes)
    chunks = range(len(sizes))
    starts = [sum(sizes[:k]) for k in chunks]
    peers = n_group * n_dp if flagged else n_dp
    grp = lax.axis_index("group")
    d = lax.axis_index("dp")
    t = lax.axis_index("tensor")
    x, c = t // 2, lax.rem(t, 2)
    sibling = {"tensor": x * 2 + (1 - c)}

    def dp_at(off):
        return {"dp": lax.rem(d + off, n_dp)}

    def peer_at(off):
        if not flagged:
            return dp_at(off)
        to = lax.rem(grp * n_dp + d + off, peers)
        return {"group": to // n_dp, "dp": lax.rem(to, n_dp)}

    def part_of(k, off):
        return pl.ds(n_dp * starts[k] + off * sizes[k], sizes[k])

    def whole_of(k):
        return pl.ds(n_dp * starts[k], n_dp * sizes[k])

    def others_of(k):
        return pl.ds(n_dp * starts[k] + sizes[k], (n_dp - 1) * sizes[k])

    def t_at(off):
        return {"tensor": lax.rem(t + off, n_t)}

    def w_copy(g, slot):
        i, h, j = g // (2 * n_j), lax.rem(g // n_j, 2), lax.rem(g, n_j)
        core = jnp.where(h == 0, 1 - c, c)
        dest = lax.rem(x + 1 + i, n_x) * 2 + core
        start = pl.multiple_of(dest * block + j * tile, tile)
        return pltpu.make_async_copy(w_hbm.at[:, pl.ds(start, tile)], wbuf.at[slot], w_sem.at[slot])

    barrier = pltpu.get_barrier_semaphore()
    for off in range(1, peers):
        pl.semaphore_signal(barrier, inc=1, device_id=peer_at(off), device_id_type=MESH)
    for off in range(1, n_t):
        pl.semaphore_signal(barrier, inc=1, device_id=t_at(off), device_id_type=MESH)

    att_load = pltpu.make_async_copy(att_hbm, att, in_sem.at[3])
    att_load.start()
    for g in range(RING):
        w_copy(jnp.int32(g), g).start()
    loads = [
        pltpu.make_async_copy(shr_hbm, shr, in_sem.at[0]),
        pltpu.make_async_copy(exp_hbm, exp, in_sem.at[1]),
        pltpu.make_async_copy(hid_hbm, hid, in_sem.at[2]),
    ]
    for load in loads:
        load.start()

    n_ad = slots.shape[1]
    square = (rows, rows)
    across = lax.broadcasted_iota(jnp.int32, square, 1)
    down = lax.broadcasted_iota(jnp.int32, square, 0)
    named = jnp.sum(
        jnp.where(across == down, idx[...].astype(F32), 0.0), axis=1, keepdims=True
    ).astype(jnp.int32)
    match = named == lax.broadcasted_iota(jnp.int32, (rows, n_ad), 1)
    slot = jnp.sum(jnp.where(match, slots[...].astype(F32), 0.0), axis=1, keepdims=True)
    owner = jnp.zeros((rows, 1), F32)
    for o in range(1, n_dp):
        owner = owner + jnp.where(slot >= float(o * n_slots), 1.0, 0.0)
    local = slot - owner * n_slots
    rel = owner - d.astype(F32)
    rel = jnp.where(rel < 0, rel + n_dp, rel)
    lane = lax.broadcasted_iota(jnp.int32, (rows, 128), 1).astype(F32)
    to_owner = lane == rel
    before = across < down
    earlier = jnp.dot(
        jnp.where(before, 1.0, 0.0).astype(BF16),
        jnp.where(to_owner, 1.0, 0.0).astype(BF16),
        preferred_element_type=F32,
    )
    place = jnp.sum(jnp.where(to_owner, earlier, 0.0), axis=1, keepdims=True)
    target = place + rel * sizes[0]
    for k in chunks[1:]:
        later = place + rel * sizes[k] + float((n_dp - 1) * starts[k])
        target = jnp.where(place >= float(starts[k]), later, target)
    target = jnp.where(place >= float(cap), -1.0, target)
    columns = lax.broadcasted_iota(jnp.int32, (rows, n_dp * cap), 1).astype(F32)
    sel[...] = jnp.where(columns == target, 1.0, 0.0).astype(BF16)
    if flagged:
        most = jnp.max(jnp.where(place >= float(cap), 1.0, 0.0), axis=0, keepdims=True)
        flags[0] = jnp.broadcast_to(most, (8, 128))
    for off in range(n_dp):
        here = jnp.where((lane == place) & (rel == float(off)), local, 0.0)
        row = jnp.broadcast_to(jnp.sum(here, axis=0, keepdims=True), (8, 128))
        if off == 0:
            metar[0] = row
        else:
            meta[off] = row

    fw = min(512, width)
    order = sorted(range(1, n_dp), key=lambda off: -min(off, n_dp - off))

    def f_copy(k, off):
        return pltpu.make_async_remote_copy(
            src_ref=hold.at[part_of(k, off)], dst_ref=recv.at[part_of(k, off)],
            send_sem=f_ss.at[k, off], recv_sem=f_rs.at[k, off],
            device_id=dp_at(off), device_id_type=MESH,
        )

    def m_copy(off):
        return pltpu.make_async_remote_copy(
            src_ref=meta.at[off], dst_ref=metar.at[off],
            send_sem=m_ss.at[off], recv_sem=m_rs.at[off],
            device_id=dp_at(off), device_id_type=MESH,
        )

    def z_copy(k, off):
        return pltpu.make_async_remote_copy(
            src_ref=zs.at[whole_of(k)], dst_ref=zr.at[off, whole_of(k)],
            send_sem=z_ss.at[k, off], recv_sem=z_rs.at[k, off],
            device_id=t_at(off), device_id_type=MESH,
        )

    def r_copy(k, off):
        return pltpu.make_async_remote_copy(
            src_ref=dl.at[part_of(k, off)], dst_ref=ret.at[part_of(k, off)],
            send_sem=r_ss.at[k, off], recv_sem=r_rs.at[k, off],
            device_id=dp_at(n_dp - off), device_id_type=MESH,
        )

    def o_copy(off):
        return pltpu.make_async_remote_copy(
            src_ref=flags.at[0], dst_ref=flags.at[off],
            send_sem=o_ss.at[off], recv_sem=o_rs.at[off],
            device_id=peer_at(off), device_id_type=MESH,
        )

    def p_copy(i):
        return pltpu.make_async_remote_copy(
            src_ref=psend.at[i], dst_ref=precv.at[i],
            send_sem=p_ss.at[i], recv_sem=p_rs.at[i],
            device_id=sibling, device_id_type=MESH,
        )

    def x_copy(i):
        return pltpu.make_async_remote_copy(
            src_ref=xsend.at[i], dst_ref=xrecv.at[i],
            send_sem=x_ss.at[i], recv_sem=x_rs.at[i],
            device_id={"tensor": lax.rem(x + 1 + i, n_x) * 2 + c}, device_id_type=MESH,
        )

    att_load.wait()
    for k in chunks:
        own_rows, other_rows = sizes[k], others_of(k)
        for f in range(width // fw):
            cols = pl.ds(f * fw, fw)
            part = lax.dot_general(
                sel[:, whole_of(k)], att[:, cols], (((0,), (0,)), ((), ())),
                preferred_element_type=F32,
            ).astype(BF16)
            recv[part_of(k, 0), cols] = part[:own_rows]
            hold[other_rows, cols] = part[own_rows:]
        if k == 0:
            pl.semaphore_wait(barrier, peers + n_t - 2)
            for off in order:
                m_copy(off).start()
        for off in order:
            f_copy(k, off).start()
    if flagged:
        for off in range(1, peers):
            o_copy(off).start()

    tiles = n_t * n_j

    def product(g):
        at = lax.rem(g, RING)
        w_copy(g, at).wait()
        part = jnp.dot(att[...], wbuf[at], preferred_element_type=F32)

        return part, at

    def refill(g, at):
        @pl.when(g + RING < tiles)
        def _():
            w_copy(g + RING, at).start()

    def blocks(i):
        def first(j, carry):
            g = i * 2 * n_j + j
            part, at = product(g)
            psend[i, j] = part
            refill(g, at)
            return carry

        lax.fori_loop(0, n_j, first, 0)
        p_copy(i).start()

        def second(j, carry):
            g = i * 2 * n_j + n_j + j
            part, at = product(g)
            own[i, j] = part
            refill(g, at)
            return carry

        lax.fori_loop(0, n_j, second, 0)
        p_copy(i).wait_recv()

    def far(i, carry):
        blocks(i)

        def add(j, inner):
            xsend[i, j] = (own[i, j] + precv[i, j]).astype(BF16)
            return inner

        lax.fori_loop(0, n_j, add, 0)
        x_copy(i).start()
        return carry

    lax.fori_loop(0, n_x - 1, far, 0)
    blocks(jnp.int32(n_x - 1))

    for load in loads:
        load.wait()
    for off in order:
        m_copy(off).wait_recv()
    n_q = store // 128
    per = 128 // per_slot
    halves = (lax.broadcasted_iota(jnp.int32, (n_dp * cap, 128), 1) // per_slot).astype(F32)
    for k in chunks:
        ch = sizes[k]
        r_i = lax.broadcasted_iota(jnp.int32, (ch, 128), 0) + starts[k]
        pick = lax.broadcasted_iota(jnp.int32, (ch, 128), 1) == r_i
        for off in range(n_dp):
            col = jnp.sum(jnp.where(pick, metar[off, 0:1, :], 0.0), axis=1, keepdims=True)
            slc[part_of(k, off)] = jnp.broadcast_to(col, (ch, 128))

    for k in chunks:
        ch, wide, here = sizes[k], n_dp * sizes[k], whole_of(k)
        half = halves[:wide]
        slot_of = slc[here]
        for off in order:
            f_copy(k, off).wait_recv()
        y = lax.dot_general(
            recv[here], shr[...], (((1,), (1,)), ((), ())), preferred_element_type=F32
        )
        z = jnp.zeros((wide, 128), F32)
        for q in range(n_q):
            z = z + jnp.where(slot_of == half + float(q * per), y[:, q * 128 : (q + 1) * 128], 0.0)
        zs[here] = z
        for off in range(1, n_t):
            z_copy(k, off).start()
        for off in range(1, n_t):
            z_copy(k, off).wait_recv()
        total = zs[here]
        for off in range(1, n_t):
            total = total + zr[off, here]
        spread = [
            jnp.where(slot_of == half + float(q * per), total, 0.0).astype(BF16) for q in range(n_q)
        ]
        lhs = jnp.concatenate(spread, axis=1)
        for f in range(width // fw):
            cols = pl.ds(f * fw, fw)
            part = jnp.dot(lhs, exp[:, cols], preferred_element_type=F32).astype(BF16)
            ret[part_of(k, 0), cols] = part[:ch]
            dl[others_of(k), cols] = part[ch:]
        for off in order:
            r_copy(k, off).start()

    for i in range(n_x - 1):
        x_copy(i).wait_recv()
    for j in range(n_j):
        cols = pl.ds(j * tile, tile)
        total = own[n_x - 1, j] + precv[n_x - 1, j]
        for i in range(n_x - 1):
            total = total + xrecv[i, j].astype(F32)
        own[n_x - 1, j] = hid[:, cols].astype(F32) + total

    if flagged:
        most = flags[0]
        for off in range(1, peers):
            o_copy(off).wait_recv()
            most = jnp.maximum(most, flags[off])
        over[...] = most
    else:
        over[...] = jnp.zeros((8, 128), F32)
    for k in chunks:
        for off in order:
            r_copy(k, off).wait_recv()
    for j in range(n_j):
        cols = pl.ds(j * tile, tile)
        delta = jnp.dot(sel[...], ret[:, cols], preferred_element_type=F32)
        out[:, cols] = (own[n_x - 1, j] + delta).astype(BF16)

    for off in order:
        m_copy(off).wait_send()
        for k in chunks:
            f_copy(k, off).wait_send()
            r_copy(k, off).wait_send()
    for k in chunks:
        for off in range(1, n_t):
            z_copy(k, off).wait_send()
    if flagged:
        for off in range(1, peers):
            o_copy(off).wait_send()
    for i in range(n_x):
        p_copy(i).wait_send()
    for i in range(n_x - 1):
        x_copy(i).wait_send()


def solution(mesh):
    n_group, n_dp, n_t = mesh.shape["group"], mesh.shape["dp"], mesh.shape["tensor"]
    n_x = n_t // 2

    def run(sizes, flagged, attended, hidden, weight, shrink, expand, row_adapter, store_slot):
        rows, width = attended.shape
        n_slots, rank, _ = shrink.shape
        cap = sum(sizes)
        lanes = n_dp * cap
        peers = n_group * n_dp
        depth, total = weight.shape
        block = total // n_t
        tile = min(512, block)
        n_j = block // tile
        any_space = pl.BlockSpec(memory_space=pl.ANY)
        vmem = pl.BlockSpec(memory_space=pltpu.VMEM)
        dma = pltpu.SemaphoreType.DMA
        return pl.pallas_call(
            functools.partial(kernel, n_group, n_dp, n_t, n_slots, sizes, flagged),
            out_shape=(
                jax.ShapeDtypeStruct((rows, width), BF16), jax.ShapeDtypeStruct((8, 128), F32)
            ),
            in_specs=[vmem, vmem] + [any_space] * 5,
            out_specs=(vmem, vmem),
            scratch_shapes=[
                pltpu.VMEM((rows, width), BF16),
                pltpu.VMEM((peers, 8, 128), F32),
                pltpu.VMEM((rows, lanes), BF16),
                pltpu.VMEM((lanes, width), BF16),
                pltpu.VMEM((lanes, width), BF16),
                pltpu.VMEM((n_dp, 8, 128), F32),
                pltpu.VMEM((n_dp, 8, 128), F32),
                pltpu.VMEM((lanes, 128), F32),
                pltpu.VMEM((lanes, 128), F32),
                pltpu.VMEM((n_t, lanes, 128), F32),
                pltpu.VMEM((lanes, width), BF16),
                pltpu.VMEM((lanes, width), BF16),
                pltpu.VMEM((RING, depth, tile), BF16),
                pltpu.VMEM((n_x, n_j, rows, tile), F32),
                pltpu.VMEM((n_x, n_j, rows, tile), F32),
                pltpu.VMEM((n_x, n_j, rows, tile), F32),
                pltpu.VMEM((n_x - 1, n_j, rows, tile), BF16),
                pltpu.VMEM((n_x - 1, n_j, rows, tile), BF16),
                pltpu.VMEM((rows, width), BF16),
                pltpu.VMEM((n_slots * rank, width), BF16),
                pltpu.VMEM((n_slots * rank, width), BF16),
                dma((RING,)), dma((4,)),
                dma((len(sizes), n_dp)), dma((len(sizes), n_dp)), dma((n_dp,)), dma((n_dp,)),
                dma((len(sizes), n_t)), dma((len(sizes), n_t)), dma((len(sizes), n_dp)), dma((len(sizes), n_dp)),
                dma((n_x,)), dma((n_x,)), dma((n_x,)), dma((n_x,)),
                dma((peers,)), dma((peers,)),
            ],
            compiler_params=pltpu.CompilerParams(
                collective_id=0 if flagged else 1,
                has_side_effects=True,
                vmem_limit_bytes=60 * 1024 * 1024,
            ),
        )(
            row_adapter.reshape(1, -1), store_slot.reshape(1, -1), attended, hidden, weight,
            shrink.reshape(n_slots * rank, width), expand.reshape(n_slots * rank, width),
        )

    def per_device(*blocks):
        bound = blocks[3].shape[0] * ADAPTER_ROW_CAP
        most = (bound // 2, bound // 4)
        mixed, over = run(most, True, *blocks)
        return lax.cond(
            over[0, 0] > 0.5,
            lambda: run((bound // 2, bound // 2), False, *blocks)[0],
            lambda: mixed,
        )

    placed = (
        P(("group", "dp"), "tensor"),
        P(("group", "dp"), "tensor"),
        P("tensor", None),
        P(("group", "dp"), None, "tensor"),
        P(("group", "dp"), None, "tensor"),
        P(("group", "dp"), None),
        P("group"),
    )
    return jax.shard_map(
        per_device,
        mesh=mesh,
        in_specs=placed,
        out_specs=P(("group", "dp"), "tensor"),
        check_vma=False,
    )
```

```python
import functools

import jax
import jax.numpy as jnp
from jax import lax
from jax.experimental import pallas as pl
from jax.experimental.pallas import tpu as pltpu
from jax.sharding import PartitionSpec as P

MESH = pl.DeviceIdType.MESH
ADAPTER_ROW_CAP = 8
RING = 4
F32 = jnp.float32
BF16 = jnp.bfloat16


def kernel(
    n_group, n_dp, n_t, n_slots, sizes, flagged,
    idx, slots, att_hbm, hid_hbm, w_hbm, shr_hbm, exp_hbm,
    out, over,
    att, flags, sel, hold, recv, meta, metar, slc, zs, zr, dl, ret,
    wbuf, psend, precv, own, xsend, xrecv, hid, shr, exp,
    w_sem, in_sem, f_ss, f_rs, m_ss, m_rs, z_ss, z_rs, r_ss, r_rs, p_ss, p_rs, x_ss, x_rs, o_ss, o_rs,
):
    rows, width = att.shape
    store = shr.shape[0]
    n_x = n_t // 2
    n_j, tile = own.shape[1], own.shape[3]
    block = n_j * tile
    per_slot = store // n_slots
    cap = sum(sizes)
    chunks = range(len(sizes))
    starts = [sum(sizes[:k]) for k in chunks]
    peers = n_group * n_dp if flagged else n_dp
    grp = lax.axis_index("group")
    d = lax.axis_index("dp")
    t = lax.axis_index("tensor")
    x, c = t // 2, lax.rem(t, 2)
    sibling = {"tensor": x * 2 + (1 - c)}

    def dp_at(off):
        return {"dp": lax.rem(d + off, n_dp)}

    def peer_at(off):
        if not flagged:
            return dp_at(off)
        to = lax.rem(grp * n_dp + d + off, peers)
        return {"group": to // n_dp, "dp": lax.rem(to, n_dp)}

    def part_of(k, off):
        return pl.ds(n_dp * starts[k] + off * sizes[k], sizes[k])

    def whole_of(k):
        return pl.ds(n_dp * starts[k], n_dp * sizes[k])

    def others_of(k):
        return pl.ds(n_dp * starts[k] + sizes[k], (n_dp - 1) * sizes[k])

    def t_at(off):
        return {"tensor": lax.rem(t + off, n_t)}

    def w_copy(g, slot):
        i, h, j = g // (2 * n_j), lax.rem(g // n_j, 2), lax.rem(g, n_j)
        core = jnp.where(h == 0, 1 - c, c)
        dest = lax.rem(x + 1 + i, n_x) * 2 + core
        start = pl.multiple_of(dest * block + j * tile, tile)
        return pltpu.make_async_copy(w_hbm.at[:, pl.ds(start, tile)], wbuf.at[slot], w_sem.at[slot])

    barrier = pltpu.get_barrier_semaphore()
    for off in range(1, peers):
        pl.semaphore_signal(barrier, inc=1, device_id=peer_at(off), device_id_type=MESH)
    for off in range(1, n_t):
        pl.semaphore_signal(barrier, inc=1, device_id=t_at(off), device_id_type=MESH)

    att_load = pltpu.make_async_copy(att_hbm, att, in_sem.at[3])
    att_load.start()
    for g in range(RING):
        w_copy(jnp.int32(g), g).start()
    loads = [
        pltpu.make_async_copy(shr_hbm, shr, in_sem.at[0]),
        pltpu.make_async_copy(exp_hbm, exp, in_sem.at[1]),
        pltpu.make_async_copy(hid_hbm, hid, in_sem.at[2]),
    ]
    for load in loads:
        load.start()

    n_ad = slots.shape[1]
    square = (rows, rows)
    across = lax.broadcasted_iota(jnp.int32, square, 1)
    down = lax.broadcasted_iota(jnp.int32, square, 0)
    named = jnp.sum(
        jnp.where(across == down, idx[...].astype(F32), 0.0), axis=1, keepdims=True
    ).astype(jnp.int32)
    match = named == lax.broadcasted_iota(jnp.int32, (rows, n_ad), 1)
    slot = jnp.sum(jnp.where(match, slots[...].astype(F32), 0.0), axis=1, keepdims=True)
    owner = jnp.zeros((rows, 1), F32)
    for o in range(1, n_dp):
        owner = owner + jnp.where(slot >= float(o * n_slots), 1.0, 0.0)
    local = slot - owner * n_slots
    rel = owner - d.astype(F32)
    rel = jnp.where(rel < 0, rel + n_dp, rel)
    lane = lax.broadcasted_iota(jnp.int32, (rows, 128), 1).astype(F32)
    to_owner = lane == rel
    before = across < down
    earlier = jnp.dot(
        jnp.where(before, 1.0, 0.0).astype(BF16),
        jnp.where(to_owner, 1.0, 0.0).astype(BF16),
        preferred_element_type=F32,
    )
    place = jnp.sum(jnp.where(to_owner, earlier, 0.0), axis=1, keepdims=True)
    target = place + rel * sizes[0]
    for k in chunks[1:]:
        later = place + rel * sizes[k] + float((n_dp - 1) * starts[k])
        target = jnp.where(place >= float(starts[k]), later, target)
    target = jnp.where(place >= float(cap), -1.0, target)
    columns = lax.broadcasted_iota(jnp.int32, (rows, n_dp * cap), 1).astype(F32)
    sel[...] = jnp.where(columns == target, 1.0, 0.0).astype(BF16)
    if flagged:
        most = jnp.max(jnp.where(place >= float(cap), 1.0, 0.0), axis=0, keepdims=True)
        flags[0] = jnp.broadcast_to(most, (8, 128))
    for off in range(n_dp):
        here = jnp.where((lane == place) & (rel == float(off)), local, 0.0)
        row = jnp.broadcast_to(jnp.sum(here, axis=0, keepdims=True), (8, 128))
        if off == 0:
            metar[0] = row
        else:
            meta[off] = row

    fw = min(512, width)
    order = sorted(range(1, n_dp), key=lambda off: -min(off, n_dp - off))

    def f_copy(k, off):
        return pltpu.make_async_remote_copy(
            src_ref=hold.at[part_of(k, off)], dst_ref=recv.at[part_of(k, off)],
            send_sem=f_ss.at[k, off], recv_sem=f_rs.at[k, off],
            device_id=dp_at(off), device_id_type=MESH,
        )

    def m_copy(off):
        return pltpu.make_async_remote_copy(
            src_ref=meta.at[off], dst_ref=metar.at[off],
            send_sem=m_ss.at[off], recv_sem=m_rs.at[off],
            device_id=dp_at(off), device_id_type=MESH,
        )

    def z_copy(k, off):
        return pltpu.make_async_remote_copy(
            src_ref=zs.at[whole_of(k)], dst_ref=zr.at[off, whole_of(k)],
            send_sem=z_ss.at[k, off], recv_sem=z_rs.at[k, off],
            device_id=t_at(off), device_id_type=MESH,
        )

    def r_copy(k, off):
        return pltpu.make_async_remote_copy(
            src_ref=dl.at[part_of(k, off)], dst_ref=ret.at[part_of(k, off)],
            send_sem=r_ss.at[k, off], recv_sem=r_rs.at[k, off],
            device_id=dp_at(n_dp - off), device_id_type=MESH,
        )

    def o_copy(off):
        return pltpu.make_async_remote_copy(
            src_ref=flags.at[0], dst_ref=flags.at[off],
            send_sem=o_ss.at[off], recv_sem=o_rs.at[off],
            device_id=peer_at(off), device_id_type=MESH,
        )

    def p_copy(i):
        return pltpu.make_async_remote_copy(
            src_ref=psend.at[i], dst_ref=precv.at[i],
            send_sem=p_ss.at[i], recv_sem=p_rs.at[i],
            device_id=sibling, device_id_type=MESH,
        )

    def x_copy(i):
        return pltpu.make_async_remote_copy(
            src_ref=xsend.at[i], dst_ref=xrecv.at[i],
            send_sem=x_ss.at[i], recv_sem=x_rs.at[i],
            device_id={"tensor": lax.rem(x + 1 + i, n_x) * 2 + c}, device_id_type=MESH,
        )

    att_load.wait()
    for k in chunks:
        own_rows, other_rows = sizes[k], others_of(k)
        for f in range(width // fw):
            cols = pl.ds(f * fw, fw)
            part = lax.dot_general(
                sel[:, whole_of(k)], att[:, cols], (((0,), (0,)), ((), ())),
                preferred_element_type=F32,
            ).astype(BF16)
            recv[part_of(k, 0), cols] = part[:own_rows]
            hold[other_rows, cols] = part[own_rows:]
        if k == 0:
            pl.semaphore_wait(barrier, peers + n_t - 2)
            for off in order:
                m_copy(off).start()
        for off in order:
            f_copy(k, off).start()
    if flagged:
        for off in range(1, peers):
            o_copy(off).start()

    tiles = n_t * n_j

    def product(g):
        at = lax.rem(g, RING)
        w_copy(g, at).wait()
        part = jnp.dot(att[...], wbuf[at], preferred_element_type=F32)

        return part, at

    def refill(g, at):
        @pl.when(g + RING < tiles)
        def _():
            w_copy(g + RING, at).start()

    def first(i):
        def step(j, carry):
            g = i * 2 * n_j + j
            part, at = product(g)
            psend[i, j] = part
            refill(g, at)
            return carry

        lax.fori_loop(0, n_j, step, 0)
        p_copy(i).start()

    def second(i):
        def step(j, carry):
            g = i * 2 * n_j + n_j + j
            part, at = product(g)
            own[i, j] = part
            refill(g, at)
            return carry

        lax.fori_loop(0, n_j, step, 0)
        p_copy(i).wait_recv()

    def far(i, carry):
        first(i)
        second(i)

        def add(j, inner):
            xsend[i, j] = (own[i, j] + precv[i, j]).astype(BF16)
            return inner

        lax.fori_loop(0, n_j, add, 0)
        return carry

    def send_far():
        for i in range(n_x - 1):
            x_copy(i).start()

    near = jnp.int32(n_x - 1)
    lax.fori_loop(0, n_x - 1, far, 0)

    for load in loads:
        load.wait()
    for off in order:
        m_copy(off).wait_recv()
    n_q = store // 128
    per = 128 // per_slot
    halves = (lax.broadcasted_iota(jnp.int32, (n_dp * cap, 128), 1) // per_slot).astype(F32)
    for k in chunks:
        ch = sizes[k]
        r_i = lax.broadcasted_iota(jnp.int32, (ch, 128), 0) + starts[k]
        pick = lax.broadcasted_iota(jnp.int32, (ch, 128), 1) == r_i
        for off in range(n_dp):
            col = jnp.sum(jnp.where(pick, metar[off, 0:1, :], 0.0), axis=1, keepdims=True)
            slc[part_of(k, off)] = jnp.broadcast_to(col, (ch, 128))

    def shrink(k):
        wide, here = n_dp * sizes[k], whole_of(k)
        half = halves[:wide]
        slot_of = slc[here]
        for off in order:
            f_copy(k, off).wait_recv()
        y = lax.dot_general(
            recv[here], shr[...], (((1,), (1,)), ((), ())), preferred_element_type=F32
        )
        z = jnp.zeros((wide, 128), F32)
        for q in range(n_q):
            z = z + jnp.where(slot_of == half + float(q * per), y[:, q * 128 : (q + 1) * 128], 0.0)
        zs[here] = z
        for off in range(1, n_t):
            z_copy(k, off).start()

    def expand(k):
        ch, wide, here = sizes[k], n_dp * sizes[k], whole_of(k)
        half = halves[:wide]
        slot_of = slc[here]
        for off in range(1, n_t):
            z_copy(k, off).wait_recv()
        total = zs[here]
        for off in range(1, n_t):
            total = total + zr[off, here]
        spread = [
            jnp.where(slot_of == half + float(q * per), total, 0.0).astype(BF16) for q in range(n_q)
        ]
        lhs = jnp.concatenate(spread, axis=1)
        for f in range(width // fw):
            cols = pl.ds(f * fw, fw)
            part = jnp.dot(lhs, exp[:, cols], preferred_element_type=F32).astype(BF16)
            ret[part_of(k, 0), cols] = part[:ch]
            dl[others_of(k), cols] = part[ch:]
        for off in order:
            r_copy(k, off).start()

    shrink(0)
    first(near)
    expand(0)
    for k in chunks[1:]:
        shrink(k)
        if k == 1:
            second(near)
        if k == chunks[-1]:
            send_far()
        expand(k)

    for i in range(n_x - 1):
        x_copy(i).wait_recv()
    for j in range(n_j):
        cols = pl.ds(j * tile, tile)
        total = own[n_x - 1, j] + precv[n_x - 1, j]
        for i in range(n_x - 1):
            total = total + xrecv[i, j].astype(F32)
        own[n_x - 1, j] = hid[:, cols].astype(F32) + total

    if flagged:
        most = flags[0]
        for off in range(1, peers):
            o_copy(off).wait_recv()
            most = jnp.maximum(most, flags[off])
        over[...] = most
    else:
        over[...] = jnp.zeros((8, 128), F32)
    for k in chunks:
        for off in order:
            r_copy(k, off).wait_recv()
        for j in range(n_j):
            cols = pl.ds(j * tile, tile)
            delta = jnp.dot(
                sel[:, whole_of(k)], ret[whole_of(k), cols], preferred_element_type=F32
            )
            total = own[n_x - 1, j] + delta
            if k == chunks[-1]:
                out[:, cols] = total.astype(BF16)
            else:
                own[n_x - 1, j] = total

    for off in order:
        m_copy(off).wait_send()
        for k in chunks:
            f_copy(k, off).wait_send()
            r_copy(k, off).wait_send()
    for k in chunks:
        for off in range(1, n_t):
            z_copy(k, off).wait_send()
    if flagged:
        for off in range(1, peers):
            o_copy(off).wait_send()
    for i in range(n_x):
        p_copy(i).wait_send()
    for i in range(n_x - 1):
        x_copy(i).wait_send()


def solution(mesh):
    n_group, n_dp, n_t = mesh.shape["group"], mesh.shape["dp"], mesh.shape["tensor"]
    n_x = n_t // 2

    def run(sizes, flagged, attended, hidden, weight, shrink, expand, row_adapter, store_slot):
        rows, width = attended.shape
        n_slots, rank, _ = shrink.shape
        cap = sum(sizes)
        lanes = n_dp * cap
        peers = n_group * n_dp
        depth, total = weight.shape
        block = total // n_t
        tile = min(512, block)
        n_j = block // tile
        any_space = pl.BlockSpec(memory_space=pl.ANY)
        vmem = pl.BlockSpec(memory_space=pltpu.VMEM)
        dma = pltpu.SemaphoreType.DMA
        return pl.pallas_call(
            functools.partial(kernel, n_group, n_dp, n_t, n_slots, sizes, flagged),
            out_shape=(
                jax.ShapeDtypeStruct((rows, width), BF16), jax.ShapeDtypeStruct((8, 128), F32)
            ),
            in_specs=[vmem, vmem] + [any_space] * 5,
            out_specs=(vmem, vmem),
            scratch_shapes=[
                pltpu.VMEM((rows, width), BF16),
                pltpu.VMEM((peers, 8, 128), F32),
                pltpu.VMEM((rows, lanes), BF16),
                pltpu.VMEM((lanes, width), BF16),
                pltpu.VMEM((lanes, width), BF16),
                pltpu.VMEM((n_dp, 8, 128), F32),
                pltpu.VMEM((n_dp, 8, 128), F32),
                pltpu.VMEM((lanes, 128), F32),
                pltpu.VMEM((lanes, 128), F32),
                pltpu.VMEM((n_t, lanes, 128), F32),
                pltpu.VMEM((lanes, width), BF16),
                pltpu.VMEM((lanes, width), BF16),
                pltpu.VMEM((RING, depth, tile), BF16),
                pltpu.VMEM((n_x, n_j, rows, tile), F32),
                pltpu.VMEM((n_x, n_j, rows, tile), F32),
                pltpu.VMEM((n_x, n_j, rows, tile), F32),
                pltpu.VMEM((n_x - 1, n_j, rows, tile), BF16),
                pltpu.VMEM((n_x - 1, n_j, rows, tile), BF16),
                pltpu.VMEM((rows, width), BF16),
                pltpu.VMEM((n_slots * rank, width), BF16),
                pltpu.VMEM((n_slots * rank, width), BF16),
                dma((RING,)), dma((4,)),
                dma((len(sizes), n_dp)), dma((len(sizes), n_dp)), dma((n_dp,)), dma((n_dp,)),
                dma((len(sizes), n_t)), dma((len(sizes), n_t)), dma((len(sizes), n_dp)), dma((len(sizes), n_dp)),
                dma((n_x,)), dma((n_x,)), dma((n_x,)), dma((n_x,)),
                dma((peers,)), dma((peers,)),
            ],
            compiler_params=pltpu.CompilerParams(
                collective_id=0 if flagged else 1,
                has_side_effects=True,
                vmem_limit_bytes=60 * 1024 * 1024,
            ),
        )(
            row_adapter.reshape(1, -1), store_slot.reshape(1, -1), attended, hidden, weight,
            shrink.reshape(n_slots * rank, width), expand.reshape(n_slots * rank, width),
        )

    def per_device(*blocks):
        bound = blocks[3].shape[0] * ADAPTER_ROW_CAP
        most = (bound // 4, bound // 2)
        mixed, over = run(most, True, *blocks)
        return lax.cond(
            over[0, 0] > 0.5,
            lambda: run((bound // 2, bound // 2), False, *blocks)[0],
            lambda: mixed,
        )

    placed = (
        P(("group", "dp"), "tensor"),
        P(("group", "dp"), "tensor"),
        P("tensor", None),
        P(("group", "dp"), None, "tensor"),
        P(("group", "dp"), None, "tensor"),
        P(("group", "dp"), None),
        P("group"),
    )
    return jax.shard_map(
        per_device,
        mesh=mesh,
        in_specs=placed,
        out_specs=P(("group", "dp"), "tensor"),
        check_vma=False,
    )
```

```python
import functools

import jax
import jax.numpy as jnp
from jax import lax
from jax.experimental import pallas as pl
from jax.experimental.pallas import tpu as pltpu
from jax.sharding import PartitionSpec as P

MESH = pl.DeviceIdType.MESH
ADAPTER_ROW_CAP = 8
RING = 4
F32 = jnp.float32
BF16 = jnp.bfloat16


def kernel(
    n_group, n_dp, n_t, n_slots, sizes, flagged,
    idx, slots, att_hbm, hid_hbm, w_hbm, shr_hbm, exp_hbm,
    out, over,
    att, flags, sel, hold, recv, meta, metar, slc, zs, zr, dl, ret,
    wbuf, psend, precv, own, xsend, xrecv, hid, shr, exp,
    w_sem, in_sem, f_ss, f_rs, m_ss, m_rs, z_ss, z_rs, r_ss, r_rs, p_ss, p_rs, x_ss, x_rs, o_ss, o_rs,
):
    rows, width = att.shape
    store = shr.shape[0]
    n_x = n_t // 2
    n_j, tile = own.shape[1], own.shape[3]
    block = n_j * tile
    per_slot = store // n_slots
    cap = sum(sizes)
    chunks = range(len(sizes))
    starts = [sum(sizes[:k]) for k in chunks]
    peers = n_group * n_dp if flagged else n_dp
    grp = lax.axis_index("group")
    d = lax.axis_index("dp")
    t = lax.axis_index("tensor")
    x, c = t // 2, lax.rem(t, 2)
    sibling = {"tensor": x * 2 + (1 - c)}

    def dp_at(off):
        return {"dp": lax.rem(d + off, n_dp)}

    def peer_at(off):
        if not flagged:
            return dp_at(off)
        to = lax.rem(grp * n_dp + d + off, peers)
        return {"group": to // n_dp, "dp": lax.rem(to, n_dp)}

    def part_of(k, off):
        return pl.ds(n_dp * starts[k] + off * sizes[k], sizes[k])

    def whole_of(k):
        return pl.ds(n_dp * starts[k], n_dp * sizes[k])

    def others_of(k):
        return pl.ds(n_dp * starts[k] + sizes[k], (n_dp - 1) * sizes[k])

    def t_at(off):
        return {"tensor": lax.rem(t + off, n_t)}

    def w_copy(g, slot):
        i, h, j = g // (2 * n_j), lax.rem(g // n_j, 2), lax.rem(g, n_j)
        core = jnp.where(h == 0, 1 - c, c)
        dest = lax.rem(x + 1 + i, n_x) * 2 + core
        start = pl.multiple_of(dest * block + j * tile, tile)
        return pltpu.make_async_copy(w_hbm.at[:, pl.ds(start, tile)], wbuf.at[slot], w_sem.at[slot])

    barrier = pltpu.get_barrier_semaphore()
    for off in range(1, peers):
        pl.semaphore_signal(barrier, inc=1, device_id=peer_at(off), device_id_type=MESH)
    for off in range(1, n_t):
        pl.semaphore_signal(barrier, inc=1, device_id=t_at(off), device_id_type=MESH)

    att_load = pltpu.make_async_copy(att_hbm, att, in_sem.at[3])
    att_load.start()
    for g in range(RING):
        w_copy(jnp.int32(g), g).start()
    loads = [
        pltpu.make_async_copy(shr_hbm, shr, in_sem.at[0]),
        pltpu.make_async_copy(exp_hbm, exp, in_sem.at[1]),
        pltpu.make_async_copy(hid_hbm, hid, in_sem.at[2]),
    ]
    for load in loads:
        load.start()

    n_ad = slots.shape[1]
    square = (rows, rows)
    across = lax.broadcasted_iota(jnp.int32, square, 1)
    down = lax.broadcasted_iota(jnp.int32, square, 0)
    named = jnp.sum(
        jnp.where(across == down, idx[...].astype(F32), 0.0), axis=1, keepdims=True
    ).astype(jnp.int32)
    match = named == lax.broadcasted_iota(jnp.int32, (rows, n_ad), 1)
    slot = jnp.sum(jnp.where(match, slots[...].astype(F32), 0.0), axis=1, keepdims=True)
    owner = jnp.zeros((rows, 1), F32)
    for o in range(1, n_dp):
        owner = owner + jnp.where(slot >= float(o * n_slots), 1.0, 0.0)
    local = slot - owner * n_slots
    rel = owner - d.astype(F32)
    rel = jnp.where(rel < 0, rel + n_dp, rel)
    lane = lax.broadcasted_iota(jnp.int32, (rows, 128), 1).astype(F32)
    to_owner = lane == rel
    before = across < down
    earlier = jnp.dot(
        jnp.where(before, 1.0, 0.0).astype(BF16),
        jnp.where(to_owner, 1.0, 0.0).astype(BF16),
        preferred_element_type=F32,
    )
    place = jnp.sum(jnp.where(to_owner, earlier, 0.0), axis=1, keepdims=True)
    target = place + rel * sizes[0]
    for k in chunks[1:]:
        later = place + rel * sizes[k] + float((n_dp - 1) * starts[k])
        target = jnp.where(place >= float(starts[k]), later, target)
    target = jnp.where(place >= float(cap), -1.0, target)
    columns = lax.broadcasted_iota(jnp.int32, (rows, n_dp * cap), 1).astype(F32)
    sel[...] = jnp.where(columns == target, 1.0, 0.0).astype(BF16)
    if flagged:
        most = jnp.max(jnp.where(place >= float(cap), 1.0, 0.0), axis=0, keepdims=True)
        flags[0] = jnp.broadcast_to(most, (8, 128))
    for off in range(n_dp):
        here = jnp.where((lane == place) & (rel == float(off)), local, 0.0)
        row = jnp.broadcast_to(jnp.sum(here, axis=0, keepdims=True), (8, 128))
        if off == 0:
            metar[0] = row
        else:
            meta[off] = row

    fw = min(512, width)
    order = sorted(range(1, n_dp), key=lambda off: -min(off, n_dp - off))

    def f_copy(k, off):
        return pltpu.make_async_remote_copy(
            src_ref=hold.at[part_of(k, off)], dst_ref=recv.at[part_of(k, off)],
            send_sem=f_ss.at[k, off], recv_sem=f_rs.at[k, off],
            device_id=dp_at(off), device_id_type=MESH,
        )

    def m_copy(off):
        return pltpu.make_async_remote_copy(
            src_ref=meta.at[off], dst_ref=metar.at[off],
            send_sem=m_ss.at[off], recv_sem=m_rs.at[off],
            device_id=dp_at(off), device_id_type=MESH,
        )

    def z_copy(k, off):
        return pltpu.make_async_remote_copy(
            src_ref=zs.at[whole_of(k)], dst_ref=zr.at[off, whole_of(k)],
            send_sem=z_ss.at[k, off], recv_sem=z_rs.at[k, off],
            device_id=t_at(off), device_id_type=MESH,
        )

    def r_copy(k, off):
        return pltpu.make_async_remote_copy(
            src_ref=dl.at[part_of(k, off)], dst_ref=ret.at[part_of(k, off)],
            send_sem=r_ss.at[k, off], recv_sem=r_rs.at[k, off],
            device_id=dp_at(n_dp - off), device_id_type=MESH,
        )

    def o_copy(off):
        return pltpu.make_async_remote_copy(
            src_ref=flags.at[0], dst_ref=flags.at[off],
            send_sem=o_ss.at[off], recv_sem=o_rs.at[off],
            device_id=peer_at(off), device_id_type=MESH,
        )

    def p_copy(i):
        return pltpu.make_async_remote_copy(
            src_ref=psend.at[i], dst_ref=precv.at[i],
            send_sem=p_ss.at[i], recv_sem=p_rs.at[i],
            device_id=sibling, device_id_type=MESH,
        )

    def x_copy(i):
        return pltpu.make_async_remote_copy(
            src_ref=xsend.at[i], dst_ref=xrecv.at[i],
            send_sem=x_ss.at[i], recv_sem=x_rs.at[i],
            device_id={"tensor": lax.rem(x + 1 + i, n_x) * 2 + c}, device_id_type=MESH,
        )

    att_load.wait()
    for k in chunks:
        own_rows, other_rows = sizes[k], others_of(k)
        for f in range(width // fw):
            cols = pl.ds(f * fw, fw)
            part = lax.dot_general(
                sel[:, whole_of(k)], att[:, cols], (((0,), (0,)), ((), ())),
                preferred_element_type=F32,
            ).astype(BF16)
            recv[part_of(k, 0), cols] = part[:own_rows]
            hold[other_rows, cols] = part[own_rows:]
        if k == 0:
            pl.semaphore_wait(barrier, peers + n_t - 2)
            for off in order:
                m_copy(off).start()
        for off in order:
            f_copy(k, off).start()
    if flagged:
        for off in range(1, peers):
            o_copy(off).start()

    tiles = n_t * n_j

    def product(g):
        at = lax.rem(g, RING)
        w_copy(g, at).wait()
        part = jnp.dot(att[...], wbuf[at], preferred_element_type=F32)

        return part, at

    def refill(g, at):
        @pl.when(g + RING < tiles)
        def _():
            w_copy(g + RING, at).start()

    def first(i):
        def step(j, carry):
            g = i * 2 * n_j + j
            part, at = product(g)
            psend[i, j] = part
            refill(g, at)
            return carry

        lax.fori_loop(0, n_j, step, 0)
        p_copy(i).start()

    def second(i):
        def step(j, carry):
            g = i * 2 * n_j + n_j + j
            part, at = product(g)
            own[i, j] = part
            refill(g, at)
            return carry

        lax.fori_loop(0, n_j, step, 0)
        p_copy(i).wait_recv()

    def far(i, carry):
        first(i)
        second(i)

        def add(j, inner):
            xsend[i, j] = (own[i, j] + precv[i, j]).astype(BF16)
            return inner

        lax.fori_loop(0, n_j, add, 0)
        return carry

    def send_far():
        for i in range(n_x - 1):
            x_copy(i).start()

    near = jnp.int32(n_x - 1)
    lax.fori_loop(0, n_x - 1, far, 0)

    for load in loads:
        load.wait()
    for off in order:
        m_copy(off).wait_recv()
    n_q = store // 128
    per = 128 // per_slot
    halves = (lax.broadcasted_iota(jnp.int32, (n_dp * cap, 128), 1) // per_slot).astype(F32)
    for k in chunks:
        ch = sizes[k]
        r_i = lax.broadcasted_iota(jnp.int32, (ch, 128), 0) + starts[k]
        pick = lax.broadcasted_iota(jnp.int32, (ch, 128), 1) == r_i
        for off in range(n_dp):
            col = jnp.sum(jnp.where(pick, metar[off, 0:1, :], 0.0), axis=1, keepdims=True)
            slc[part_of(k, off)] = jnp.broadcast_to(col, (ch, 128))

    def shrink(k):
        wide, here = n_dp * sizes[k], whole_of(k)
        half = halves[:wide]
        slot_of = slc[here]
        for off in order:
            f_copy(k, off).wait_recv()
        y = lax.dot_general(
            recv[here], shr[...], (((1,), (1,)), ((), ())), preferred_element_type=F32
        )
        z = jnp.zeros((wide, 128), F32)
        for q in range(n_q):
            z = z + jnp.where(slot_of == half + float(q * per), y[:, q * 128 : (q + 1) * 128], 0.0)
        zs[here] = z
        for off in range(1, n_t):
            z_copy(k, off).start()

    def expand(k):
        ch, wide, here = sizes[k], n_dp * sizes[k], whole_of(k)
        half = halves[:wide]
        slot_of = slc[here]
        for off in range(1, n_t):
            z_copy(k, off).wait_recv()
        total = zs[here]
        for off in range(1, n_t):
            total = total + zr[off, here]
        spread = [
            jnp.where(slot_of == half + float(q * per), total, 0.0).astype(BF16) for q in range(n_q)
        ]
        lhs = jnp.concatenate(spread, axis=1)
        for f in range(width // fw):
            cols = pl.ds(f * fw, fw)
            part = jnp.dot(lhs, exp[:, cols], preferred_element_type=F32).astype(BF16)
            ret[part_of(k, 0), cols] = part[:ch]
            dl[others_of(k), cols] = part[ch:]
        for off in order:
            r_copy(k, off).start()

    shrink(0)
    first(near)
    expand(0)
    for k in chunks[1:]:
        shrink(k)
        if k == 1:
            second(near)
        if k == chunks[-1]:
            send_far()
        expand(k)

    for i in range(n_x - 1):
        x_copy(i).wait_recv()
    for j in range(n_j):
        cols = pl.ds(j * tile, tile)
        total = own[n_x - 1, j] + precv[n_x - 1, j]
        for i in range(n_x - 1):
            total = total + xrecv[i, j].astype(F32)
        own[n_x - 1, j] = hid[:, cols].astype(F32) + total

    if flagged:
        most = flags[0]
        for off in range(1, peers):
            o_copy(off).wait_recv()
            most = jnp.maximum(most, flags[off])
        over[0, 0] = jnp.max(most)
    else:
        over[0, 0] = jnp.float32(0.0)
    for k in chunks:
        for off in order:
            r_copy(k, off).wait_recv()
        for j in range(n_j):
            cols = pl.ds(j * tile, tile)
            delta = jnp.dot(
                sel[:, whole_of(k)], ret[whole_of(k), cols], preferred_element_type=F32
            )
            total = own[n_x - 1, j] + delta
            if k == chunks[-1]:
                out[:, cols] = total.astype(BF16)
            else:
                own[n_x - 1, j] = total

    for off in order:
        m_copy(off).wait_send()
        for k in chunks:
            f_copy(k, off).wait_send()
            r_copy(k, off).wait_send()
    for k in chunks:
        for off in range(1, n_t):
            z_copy(k, off).wait_send()
    if flagged:
        for off in range(1, peers):
            o_copy(off).wait_send()
    for i in range(n_x):
        p_copy(i).wait_send()
    for i in range(n_x - 1):
        x_copy(i).wait_send()


def solution(mesh):
    n_group, n_dp, n_t = mesh.shape["group"], mesh.shape["dp"], mesh.shape["tensor"]
    n_x = n_t // 2

    def run(sizes, flagged, attended, hidden, weight, shrink, expand, row_adapter, store_slot):
        rows, width = attended.shape
        n_slots, rank, _ = shrink.shape
        cap = sum(sizes)
        lanes = n_dp * cap
        peers = n_group * n_dp
        depth, total = weight.shape
        block = total // n_t
        tile = min(512, block)
        n_j = block // tile
        any_space = pl.BlockSpec(memory_space=pl.ANY)
        vmem = pl.BlockSpec(memory_space=pltpu.VMEM)
        dma = pltpu.SemaphoreType.DMA
        return pl.pallas_call(
            functools.partial(kernel, n_group, n_dp, n_t, n_slots, sizes, flagged),
            out_shape=(
                jax.ShapeDtypeStruct((rows, width), BF16), jax.ShapeDtypeStruct((1, 1), F32)
            ),
            in_specs=[vmem, vmem] + [any_space] * 5,
            out_specs=(vmem, pl.BlockSpec(memory_space=pltpu.SMEM)),
            scratch_shapes=[
                pltpu.VMEM((rows, width), BF16),
                pltpu.VMEM((peers, 8, 128), F32),
                pltpu.VMEM((rows, lanes), BF16),
                pltpu.VMEM((lanes, width), BF16),
                pltpu.VMEM((lanes, width), BF16),
                pltpu.VMEM((n_dp, 8, 128), F32),
                pltpu.VMEM((n_dp, 8, 128), F32),
                pltpu.VMEM((lanes, 128), F32),
                pltpu.VMEM((lanes, 128), F32),
                pltpu.VMEM((n_t, lanes, 128), F32),
                pltpu.VMEM((lanes, width), BF16),
                pltpu.VMEM((lanes, width), BF16),
                pltpu.VMEM((RING, depth, tile), BF16),
                pltpu.VMEM((n_x, n_j, rows, tile), F32),
                pltpu.VMEM((n_x, n_j, rows, tile), F32),
                pltpu.VMEM((n_x, n_j, rows, tile), F32),
                pltpu.VMEM((n_x - 1, n_j, rows, tile), BF16),
                pltpu.VMEM((n_x - 1, n_j, rows, tile), BF16),
                pltpu.VMEM((rows, width), BF16),
                pltpu.VMEM((n_slots * rank, width), BF16),
                pltpu.VMEM((n_slots * rank, width), BF16),
                dma((RING,)), dma((4,)),
                dma((len(sizes), n_dp)), dma((len(sizes), n_dp)), dma((n_dp,)), dma((n_dp,)),
                dma((len(sizes), n_t)), dma((len(sizes), n_t)), dma((len(sizes), n_dp)), dma((len(sizes), n_dp)),
                dma((n_x,)), dma((n_x,)), dma((n_x,)), dma((n_x,)),
                dma((peers,)), dma((peers,)),
            ],
            compiler_params=pltpu.CompilerParams(
                collective_id=0 if flagged else 1,
                has_side_effects=True,
                vmem_limit_bytes=60 * 1024 * 1024,
            ),
        )(
            row_adapter.reshape(1, -1), store_slot.reshape(1, -1), attended, hidden, weight,
            shrink.reshape(n_slots * rank, width), expand.reshape(n_slots * rank, width),
        )

    def per_device(*blocks):
        bound = blocks[3].shape[0] * ADAPTER_ROW_CAP
        most = (bound // 4, bound // 2)
        mixed, over = run(most, True, *blocks)
        return lax.cond(
            over[0, 0] > 0.5,
            lambda: run((bound // 2, bound // 2), False, *blocks)[0],
            lambda: mixed,
        )

    placed = (
        P(("group", "dp"), "tensor"),
        P(("group", "dp"), "tensor"),
        P("tensor", None),
        P(("group", "dp"), None, "tensor"),
        P(("group", "dp"), None, "tensor"),
        P(("group", "dp"), None),
        P("group"),
    )
    return jax.shard_map(
        per_device,
        mesh=mesh,
        in_specs=placed,
        out_specs=P(("group", "dp"), "tensor"),
        check_vma=False,
    )
```
